128 devices in a mesh: atom: 16 (over x, z), aux: 8 (over y, core).
Axes of the slice: x: 4, y: 4, z: 4, core: 2. Of those that a mesh axis runs over, the one named last changes fastest.
Arguments:
- three_index: bfloat16 [256, 64, 128, 128], P('atom', 'aux'), may hold values from -6 to 6
- pair_mask: int32 [256, 8, 8], P('atom'), may hold values 0 or 1
- pair_owner: int32 [256, 1], P('atom'), may hold values from 0 to 15; in each aligned block of 16 rows (0 to 15, 16 to 31, ...) at most 2 rows name the same one
- pair_sub: int32 [256], P('atom'), may hold values from 0 to 3
- pair_nu: int32 [256], P('atom'), may hold values from 0 to 63
- live_count: int32 [16], P('atom'), may hold values from 1 to 16, 192 in all
- coefficients: bfloat16 [8192, 128], P('atom'), may hold values from -0.5 to 0.5
- fit_matrix: bfloat16 [64, 64], P('aux'), as said below
Outputs:
- exchange: float32 [8192, 8192], P('atom', 'aux')
The draws below stay inside these ranges and needn't reach their ends.
Inputs may be any that keep to these rules, and one draw needn't show every extreme that they name: `pair_owner`: among the 16 slots of one atom index, at most 2 name the same owner, and in every draw some owner is named exactly 2 times by some atom index's slots. The first live_count[a] slots of atom index a are live; some atom index has all 16 slots live. `fit_matrix`: Symmetric.
All inputs are finite; a program needn't handle non-finite values. No bound on the sum of `pair_mask` or of `live_count` on one device may be relied on, other than what follows from the above.
Results may differ from the reference program's by a relative error of at most 0.012.
Values may be sent and summed in bfloat16 or wider, within the bound.
No kernel may reach another device: no remote copies, remote signals or barrier semaphores. Data moves between devices by JAX's collectives and lax.ppermute only.
A program may use at most 128 MiB of HBM per device.

```python
import math
import jax
import jax.numpy as jnp
import numpy as np
from jax import lax

BLK = 128
AB = 8
NOCC = 128
AUX_DEV = 8
MB_DEV = 4
TASK_DEV = 16
CAP = 2
NAUX = 64
NB = 64
NBF = 8192
PAIRS = 256
N_ATOM = 16
N_AUX = 8


def draw_fit_matrix(key, part):
    first_key, second_key = jax.random.split(jax.random.fold_in(key, 17), 2)
    base = jax.random.normal(first_key, (NAUX, NAUX), jnp.float32) * NAUX ** (-0.5)
    matrix = (base + base.T) * 0.7071
    diagonal = jax.random.uniform(second_key, (NAUX,), jnp.float32, -0.5, 0.5)
    matrix = matrix + jnp.diag(diagonal)
    return matrix.astype(jnp.bfloat16)


def with_ends(result, own_key, low, largest):
    longest = result.shape.index(max(result.shape))
    spots = []
    for shift in (0, 1):
        where = [jax.random.randint(jax.random.fold_in(own_key, axis), (), 0, length) for axis, length in enumerate(result.shape)]
        where[longest] = (where[longest] + shift) % result.shape[longest]
        spots.append(tuple(where))
    return result.at[spots[0]].set(low).at[spots[1]].set(largest)


def shard_levels(own_key, shape, cuts, least, largest):
    factor_of, own = 1.0, jax.random.fold_in(own_key, 6)
    for dim, parts in cuts:
        heights = jnp.exp(jax.random.uniform(jax.random.fold_in(own, dim), (parts,), jnp.float32, least / len(cuts), largest / len(cuts)))
        factor_of = factor_of * jnp.repeat(heights, shape[dim] // parts).reshape([-1 if axis == dim else 1 for axis in range(len(shape))])
    return factor_of


def profile(amount, total, limit, lean):
    weights = [(1 << 20) // math.isqrt(rank ** lean) + 1 for rank in range(2, amount + 1)]
    surplus, holding = total - limit - (amount - 1), [1] * (amount - 1)
    while surplus > 0:
        candidates = [i for i in range(amount - 1) if holding[i] < limit]
        mass, remaining = sum([weights[i] for i in candidates]), surplus
        for i in candidates:
            more = min(limit - holding[i], max(1, remaining * weights[i] // mass), surplus)
            holding[i] = holding[i] + more
            surplus = surplus - more
    return np.array([limit] + holding)


def ragged(key, count, total, limit, skew):
    if count == 2:
        one = jax.random.randint(key, (), max(1, total - limit), min(limit, total - 1) + 1)
        return jnp.stack([one, total - one])
    lengths = jnp.asarray(profile(count, total, limit, skew), jnp.int32)
    couples = (count - 1) // 2
    donor, sink = lengths[1:1 + 2 * couples:2], lengths[2:2 + 2 * couples:2]
    slack = jnp.minimum(donor - 1, limit - sink)
    passed = jax.random.randint(jax.random.fold_in(key, 1), (couples,), 0, 1 << 20) % (slack + 1)
    lengths = lengths.at[1:1 + 2 * couples:2].set(donor - passed).at[2:2 + 2 * couples:2].set(sink + passed)
    return lengths[jax.random.permutation(jax.random.fold_in(key, 2), count)]


def shared_out(rng, own, number, rows, amount, top, limit, skew):
    ranking = jax.random.permutation(rng, amount)
    heavy_load, usual = load_shares(amount, rows * top, limit, skew, True), load_shares(amount, rows * top, limit, skew, False)
    places = jnp.arange(amount)

    def named(lengths, turn):
        used = int((lengths > 0).sum())
        fixed = max(1, used // 4)
        moved = fixed + (places - fixed + turn * (used - fixed)) % max(1, amount - fixed)
        return jnp.zeros((amount,), jnp.int32).at[ranking[jnp.where(places < fixed, places, moved)]].set(jnp.asarray(lengths, jnp.int32))

    lengths = jnp.where(number % 4 == 0, named(heavy_load, number // 4), named(usual, number - number // 4 - 1))
    mixed = jax.random.permutation(jax.random.fold_in(own, 3), amount)
    source_of, receiver = mixed[0:amount // 2 * 2:2], mixed[1:amount // 2 * 2:2]
    margin = jnp.minimum(lengths[source_of] - 1, limit - lengths[receiver]) // 2
    margin = jnp.where((source_of == ranking[0]) | (receiver == ranking[0]) | (lengths[receiver] == 0), 0, jnp.maximum(margin, 0))
    moved = jax.random.randint(jax.random.fold_in(own, 4), (amount // 2,), 0, 1 << 20) % (margin + 1)
    lengths = lengths.at[source_of].add(-moved).at[receiver].add(moved)
    labels = jnp.searchsorted(jnp.cumsum(lengths), jnp.arange(rows * top), side="right").astype(jnp.int32)
    listing = labels.reshape(top, rows).T
    listing = listing[jax.random.permutation(jax.random.fold_in(own, 1), rows)]
    turn = jax.random.randint(jax.random.fold_in(own, 2), (rows, 1), 0, top)
    return jnp.take_along_axis(listing, (jnp.arange(top)[None, :] + turn) % top, axis=1)


def load_shares(number_of, total, limit, lean, full):
    loads = [(1 << 20) // math.isqrt(standing ** lean) + 1 for standing in range(1, number_of + 1)]
    largest = limit if full else min(limit, max(-(-total // number_of), total * loads[0] // sum(loads)))
    least = 1 if total - largest >= number_of - 1 else 0
    holding, surplus = [largest] + [least] * (number_of - 1), total - largest - least * (number_of - 1)
    while surplus > 0:
        candidates = [i for i in range(1, number_of) if holding[i] < largest] or [i for i in range(1, number_of) if holding[i] < limit]
        mass, remaining = sum([loads[i] for i in candidates]), surplus
        for i in candidates:
            more = min(limit - holding[i], max(1, remaining * loads[i] // mass), surplus)
            holding[i] = holding[i] + more
            surplus = surplus - more
    return np.array(holding)


def gaussian(stream_key, dims, spread, reach, cuts=(), kind=jnp.bfloat16):
    loudness = shard_levels(stream_key, dims, cuts, -0.22, 0.18) if cuts else 1.0
    drawn = jax.random.normal(stream_key, dims, jnp.float32) * spread * loudness
    return jnp.minimum(jnp.maximum(drawn, -reach), reach).astype(kind)


def setup_inputs(seed: int = 0) -> dict:
    key_of = jax.random.split(jax.random.key(seed), 9)
    three_index = gaussian(key_of[0], (PAIRS, NAUX, BLK, BLK), 1.0, 6.0, ((0, 16), (1, 8)))
    pair_mask = with_ends((jax.random.randint(key_of[1], (PAIRS, AB, AB), 0, 4) < 3).astype(jnp.int32), jax.random.fold_in(key_of[1], 1), 0, 1)
    pair_owner_keys = jax.random.split(jax.random.fold_in(key_of[2], 1), PAIRS // TASK_DEV)
    pair_owner_turns = jax.random.permutation(jax.random.fold_in(key_of[2], 3), PAIRS // TASK_DEV)
    pair_owner = jax.vmap(lambda own, number: shared_out(jax.random.fold_in(key_of[2], 2), own, number, TASK_DEV, N_ATOM, 1, CAP, 2))(pair_owner_keys, pair_owner_turns).reshape((PAIRS, 1))
    pair_sub = with_ends(jax.random.randint(key_of[3], (PAIRS,), 0, MB_DEV), jax.random.fold_in(key_of[3], 1), 0, MB_DEV - 1).astype(jnp.int32)
    pair_nu = with_ends(jax.random.randint(key_of[4], (PAIRS,), 0, NB), jax.random.fold_in(key_of[4], 1), 0, NB - 1).astype(jnp.int32)
    live_count = ragged(key_of[5], N_ATOM, N_ATOM * TASK_DEV * 3 // 4, TASK_DEV, 2).astype(jnp.int32)
    coefficients = gaussian(key_of[6], (NBF, NOCC), BLK ** -0.5, 0.5, ((0, 16),))
    fit_matrix = draw_fit_matrix(jax.random.fold_in(key_of[8], 71), 0)
    return {"three_index": three_index, "pair_mask": pair_mask, "pair_owner": pair_owner, "pair_sub": pair_sub, "pair_nu": pair_nu, "live_count": live_count, "coefficients": coefficients, "fit_matrix": fit_matrix}


def reference(three_index, pair_mask, pair_owner, pair_sub, pair_nu, live_count, coefficients, fit_matrix):
    block_size = three_index.shape[2]
    aux_total = fit_matrix.shape[0]
    basis_total = coefficients.shape[0]
    occupied = coefficients.shape[1]
    shell_size = block_size // pair_mask.shape[1]
    slot_index = jnp.arange(three_index.shape[0], dtype=jnp.int32)
    alive_mask = (slot_index % TASK_DEV) < live_count[slot_index // TASK_DEV]
    mu_blocks = (pair_owner[:, 0] * MB_DEV + pair_sub).astype(jnp.int32)
    zero_index = jnp.zeros((), jnp.int32)

    def add_pair(summed, inputs):
        tile_data, small_mask, nu_block, mu_block, alive_flag = inputs
        expanded = jnp.repeat(jnp.repeat(small_mask, shell_size, 0), shell_size, 1).astype(jnp.float32)
        masked = tile_data.astype(jnp.float32) * expanded
        orbital_rows = lax.dynamic_slice(coefficients, ((nu_block * block_size).astype(jnp.int32), zero_index), (block_size, occupied)).astype(jnp.float32)
        halfway = jnp.einsum("pmn,ni->pmi", masked, orbital_rows)
        rounded = lax.optimization_barrier(halfway.astype(jnp.bfloat16)).astype(jnp.float32)
        rounded = jnp.where(alive_flag, rounded, 0.0)
        start_row = (mu_block * block_size).astype(jnp.int32)
        current = lax.dynamic_slice(summed, (zero_index, start_row, zero_index), (aux_total, block_size, occupied))
        return lax.dynamic_update_slice(summed, current + rounded, (zero_index, start_row, zero_index)), None

    summed, _ = lax.scan(add_pair, jnp.zeros((aux_total, basis_total, occupied), jnp.float32), (three_index, pair_mask, pair_nu, mu_blocks, alive_mask))
    half_transformed = summed.astype(jnp.bfloat16)
    flat_input = lax.optimization_barrier(half_transformed).astype(jnp.float32).reshape(aux_total, basis_total * occupied)
    fitted = jnp.dot(fit_matrix.astype(jnp.float32), flat_input).astype(jnp.bfloat16)
    left_all = half_transformed.reshape(N_AUX, AUX_DEV, basis_total, occupied)
    right_all = fitted.reshape(N_AUX, AUX_DEV, basis_total, occupied)

    def add_share(summed_exchange, pieces):
        left_piece, right_piece = pieces
        left_rows = lax.optimization_barrier(left_piece).astype(jnp.float32).transpose(1, 0, 2).reshape(basis_total, AUX_DEV * occupied)
        right_rows = lax.optimization_barrier(right_piece).astype(jnp.float32).transpose(1, 0, 2).reshape(basis_total, AUX_DEV * occupied)
        partial_value = jnp.dot(left_rows, right_rows.T)
        rounded = lax.optimization_barrier(partial_value.astype(jnp.bfloat16)).astype(jnp.float32)
        return summed_exchange + rounded, None

    exchange, _ = lax.scan(add_share, jnp.zeros((basis_total, basis_total), jnp.float32), (left_all, right_all))
    return exchange * (aux_total * occupied) ** -0.5
```

```python
import functools

import jax
import jax.numpy as jnp
from jax import lax
from jax.experimental import pallas as pl
from jax.experimental.pallas import tpu as pltpu
from jax.sharding import Mesh
from jax.sharding import PartitionSpec as P

CAP = 2
SIDE = 4
BF = jnp.bfloat16
F32 = jnp.float32
VMEM = 48 * 1024 * 1024


def shifted(value, axis, shift):
    return lax.ppermute(value, axis, [(i, (i + shift) % SIDE) for i in range(SIDE)])


def params():
    return pltpu.CompilerParams(vmem_limit_bytes=VMEM)


def cost(flops, bytes_accessed):
    return pl.CostEstimate(flops=flops, bytes_accessed=bytes_accessed, transcendentals=0)


def transform_kernel(src, valid, blk, sel, tile_ref, mask_ref, own_ref, other_ref, out_ref):
    j = pl.program_id(0)
    count = tile_ref.shape[1]

    def fill(orbitals):
        masked = tile_ref[0] * mask_ref[0][None]
        masked = masked.reshape(count * 128, 128)
        product = lax.dot_general(
            orbitals, masked, (((1,), (1,)), ((), ())), preferred_element_type=F32
        ).astype(BF)
        for p in range(count):
            out_ref[0, p] = product[:, p * 128 : (p + 1) * 128]

    @pl.when(jnp.logical_and(valid[j] > 0, sel[j] == 0))
    def _():
        fill(own_ref[blk[j]])

    @pl.when(jnp.logical_and(valid[j] > 0, sel[j] != 0))
    def _():
        fill(other_ref[blk[j]])

    @pl.when(valid[j] == 0)
    def _():
        out_ref[0] = jnp.zeros(out_ref.shape[1:], BF)


def transform(half, order, pair_nu, core, tiles, mask, own, other):
    positions = order.shape[0]
    valid = (order > 0).astype(jnp.int32)
    last = lax.cummax(jnp.where(order > 0, jnp.arange(positions), 0))
    src = jnp.maximum(order[last] - 1, 0)
    block = pair_nu[src]
    sel = jnp.where((block % 4) // 2 == core, 0, 1)
    blk = (block // 4) * 2 + block % 2
    grid_spec = pltpu.PrefetchScalarGridSpec(
        num_scalar_prefetch=4,
        grid=(positions,),
        in_specs=[
            pl.BlockSpec((1, 4, 128, 128), lambda j, src, *_: (src[j], half, 0, 0)),
            pl.BlockSpec((1, 128, 128), lambda j, src, *_: (src[j], 0, 0)),
            pl.BlockSpec((32, 128, 128), lambda j, *_: (0, 0, 0)),
            pl.BlockSpec((32, 128, 128), lambda j, *_: (0, 0, 0)),
        ],
        out_specs=pl.BlockSpec((1, 4, 128, 128), lambda j, *_: (j, 0, 0, 0)),
    )
    return pl.pallas_call(
        transform_kernel,
        grid_spec=grid_spec,
        out_shape=jax.ShapeDtypeStruct((positions, 4, 128, 128), BF),
        compiler_params=params(),
        cost_estimate=cost(2 * 16 * 4 * 128**3, 8 * 2**20),
        name="transform",
    )(src, valid, blk, sel, tiles, mask, own, other)


def collect_kernel(codes, place, a_ref, b_ref, c_ref, d_ref, out_ref, acc):
    j = pl.program_id(0)
    acc[...] = jnp.zeros(acc.shape, F32)
    for k, ref in enumerate((a_ref, b_ref, c_ref, d_ref)):
        for r in range(CAP):
            code = codes[(k * SIDE + j) * CAP + r]

            @pl.when(code > 0)
            def _(ref=ref, r=r, code=code):
                acc[code - 1] += ref[0, r].astype(F32)

    for s in range(4):
        out_ref[0, :, :, s * 128 : (s + 1) * 128] = acc[s].astype(BF)


def collect(codes, place, pieces, offsets):
    block = (1, CAP, 4, 128, 128)
    specs = [
        pl.BlockSpec(block, functools.partial(lambda o, j, *_: (o + j, 0, 0, 0, 0), o))
        for o in offsets
    ]
    grid_spec = pltpu.PrefetchScalarGridSpec(
        num_scalar_prefetch=2,
        grid=(SIDE,),
        in_specs=specs,
        out_specs=pl.BlockSpec((1, 4, 128, 512), lambda j, codes, place: (place[j], 0, 0, 0)),
        scratch_shapes=[pltpu.VMEM((4, 4, 128, 128), F32)],
    )
    return pl.pallas_call(
        collect_kernel,
        grid_spec=grid_spec,
        out_shape=jax.ShapeDtypeStruct((SIDE, 4, 128, 512), BF),
        compiler_params=params(),
        cost_estimate=cost(2**22, 6 * 2**20),
        name="collect",
    )(codes, place, *pieces)


def finish_kernel(*refs):
    out_ref = refs[-1]
    for half in range(2):
        total = refs[4 * half][0].astype(F32)
        for k in range(1, 4):
            total += refs[4 * half + k][0].astype(F32)
        out_ref[0, 4 * half : 4 * half + 4] = total.astype(BF)


def finish(pieces, offsets):
    specs = [
        pl.BlockSpec((1, 4, 16, 512), functools.partial(lambda o, g: (o, 0, g, 0), o))
        for o in offsets
    ]
    return pl.pallas_call(
        finish_kernel,
        grid=(8,),
        in_specs=specs,
        out_specs=pl.BlockSpec((1, 8, 16, 512), lambda g: (g, 0, 0, 0)),
        out_shape=jax.ShapeDtypeStruct((8, 8, 16, 512), BF),
        compiler_params=params(),
        cost_estimate=cost(2**21, 5 * 2**20),
        name="finish",
    )(*pieces)


def product_kernel(has_add, zsel, psel, left_ref, f0, f1, f2, f3, *rest):
    out_ref = rest[-1]
    x2 = pl.program_id(1)
    for s, ref in enumerate((f0, f1, f2, f3)):

        @pl.when(psel[x2] == s)
        def _(ref=ref):
            value = jnp.dot(left_ref[0], ref[...], preferred_element_type=F32)
            if has_add:
                value += rest[0][0, 0].astype(F32)
            out_ref[0, 0] = value.astype(BF)


def product(zsel, psel, left, columns, add=None):
    whole = pl.BlockSpec((1024, 512), lambda l, x2, *_: (0, 0))
    tile = pl.BlockSpec((1, 1, 512, 512), lambda l, x2, *_: (x2, l, 0, 0))
    specs = [pl.BlockSpec((1, 512, 1024), lambda l, x2, zsel, psel: (zsel[l], 0, 0))] + [whole] * 4
    operands = [left, *columns]
    if add is not None:
        specs.append(tile)
        operands.append(add)
    grid_spec = pltpu.PrefetchScalarGridSpec(
        num_scalar_prefetch=2, grid=(2, SIDE), in_specs=specs, out_specs=tile
    )
    return pl.pallas_call(
        functools.partial(product_kernel, add is not None),
        grid_spec=grid_spec,
        out_shape=jax.ShapeDtypeStruct((SIDE, 2, 512, 512), BF),
        compiler_params=params(),
        cost_estimate=cost(8 * 2 * 512 * 512 * 1024, 10 * 2**20),
        name="product",
    )(zsel, psel, *operands)


def per_device(
    three_index, pair_mask, pair_owner, pair_sub, pair_nu, live_count, coefficients, fit_matrix
):
    slots = three_index.shape[0]
    x, z, y, c = (lax.axis_index(name) for name in ("x", "z", "y", "c"))

    blocks = coefficients.reshape(4, 128, 128).transpose(0, 2, 1)
    half_blocks = lax.dynamic_slice_in_dim(blocks, c * 2, 2, 0)
    own = lax.all_to_all(
        jnp.broadcast_to(half_blocks[None], (16, 2, 128, 128)), ("x", "z"), 0, 0, tiled=True
    ).reshape(32, 128, 128)
    other = lax.ppermute(own, "c", [(0, 1), (1, 0)])

    alive = jnp.arange(slots) < live_count[0]
    code = jnp.where(alive, pair_owner[:, 0] * 4 + pair_sub, -1).astype(jnp.int32)
    codes = lax.all_gather(code, ("x", "z"), axis=0, tiled=True).reshape(16, slots)

    def table(code, value):
        owner = jnp.where(code >= 0, code // 4, -1)
        hits = (owner[..., None] == jnp.arange(16)).astype(jnp.int32)
        rank = jnp.sum(
            (owner[..., None, :] == owner[..., :, None])
            & (jnp.arange(slots)[None, :] < jnp.arange(slots)[:, None]),
            -1,
        )
        ranks = (rank[..., None] == jnp.arange(CAP)).astype(jnp.int32)
        return jnp.sum(
            hits[..., :, None] * ranks[..., None, :] * value[..., None, None], -3
        )

    outgoing = table(code, jnp.arange(1, slots + 1, dtype=jnp.int32)).reshape(4, 4, CAP)
    arriving = table(codes, codes % 4 + 1).reshape(4, 4, 4, 4, CAP)
    order_a = outgoing.transpose(1, 0, 2).reshape(-1)
    order_b = outgoing[(x + jnp.arange(4)) % 4].reshape(-1)
    codes_a = arriving[x][:, :, z].reshape(-1)
    codes_b = arriving[:, z, x][(x - jnp.arange(4)) % 4].reshape(-1)

    mask = jnp.repeat(jnp.repeat(pair_mask, 16, 1), 16, 2).astype(BF)

    out_a = transform(0, order_a, pair_nu, c, three_index, mask, own, other)
    got_a = lax.all_to_all(
        out_a.reshape(4, 8, 4, 128, 128), "z", 0, 0, tiled=True
    ).reshape(16, CAP, 4, 128, 128)
    out_b = transform(1, order_b, pair_nu, c, three_index, mask, own, other)
    out_b = out_b.reshape(4, 4, CAP, 4, 128, 128)
    got_b = [out_b[0]] + [shifted(out_b[s], "x", s) for s in (1, 2, 3)]
    sum_a = collect(codes_a, jnp.arange(4, dtype=jnp.int32), [got_a] * 4, (0, 4, 8, 12))
    last_a = lax.all_to_all(sum_a, "x", 0, 0, tiled=True)
    sum_b = collect(codes_b, ((jnp.arange(4) - z) % 4).astype(jnp.int32), got_b, (0,) * 4)
    last_b = [sum_b[:1]] + [shifted(sum_b[s : s + 1], "z", s) for s in (1, 2, 3)]
    cut = finish([last_a] * 4 + last_b, (0, 1, 2, 3, 0, 0, 0, 0))

    rows = lax.all_to_all(cut, ("y", "c"), 0, 0, tiled=True).reshape(1024, 512)

    fit = lax.all_gather(fit_matrix, ("y", "c"), axis=0, tiled=True)
    spread = (jnp.arange(1024)[:, None] // 16 == jnp.arange(64)[None, :]).astype(BF)
    mixing = jnp.dot(jnp.dot(spread, fit, preferred_element_type=F32).astype(BF), spread.T)
    same = jnp.arange(1024)[:, None] % 16 == jnp.arange(1024)[None, :] % 16
    mixing = jnp.where(same, mixing, 0).astype(BF)

    fitted = jnp.dot(mixing, rows, preferred_element_type=F32).astype(BF)
    left = lax.all_to_all(
        jnp.broadcast_to(rows.T[None], (4, 512, 1024)), "z", 0, 0, tiled=True
    )
    columns = [fitted] + [shifted(fitted, "x", s) for s in (1, 2, 3)]

    psel = ((x - jnp.arange(4)) % 4).astype(jnp.int32)
    pair = jnp.arange(2, dtype=jnp.int32)
    theirs = product(2 * (1 - c) + pair, psel, left, columns)
    theirs = lax.ppermute(theirs, "c", [(0, 1), (1, 0)])
    partial = product(2 * c + pair, psel, left, columns, theirs)

    parts = lax.all_to_all(partial, "y", 0, 0, tiled=True)
    got = []
    for t in range(2):
        tile = lax.dynamic_index_in_dim(parts, (z + t) % 2, 1, keepdims=False)
        tile = jnp.sum(tile.astype(F32), 0).astype(BF)
        pairs = [
            (zz * 2 + k, (2 * k + (zz + t) % 2) * 2 + zz // 2) for zz in range(4) for k in range(2)
        ]
        got.append(lax.ppermute(tile, ("z", "c"), pairs).astype(F32))
    scale = 8192 ** (-0.5)
    even = z % 2 == 0
    first = jnp.where(even, got[0], got[1]) * scale
    second = jnp.where(even, got[1], got[0]) * scale
    return jnp.concatenate([first, second], 1)


def solution(mesh):
    grid = Mesh(mesh.devices.reshape(4, 4, 4, 2), ("x", "z", "y", "c"))
    atom, aux = ("x", "z"), ("y", "c")
    in_specs = (
        P(atom, aux, None, None),
        P(atom, None, None),
        P(atom, None),
        P(atom),
        P(atom),
        P(atom),
        P(atom, None),
        P(aux, None),
    )
    return jax.shard_map(
        per_device, mesh=grid, in_specs=in_specs, out_specs=P(atom, aux), check_vma=False
    )
```

```python
import functools

import jax
import jax.numpy as jnp
from jax import lax
from jax.experimental import pallas as pl
from jax.experimental.pallas import tpu as pltpu
from jax.sharding import Mesh
from jax.sharding import PartitionSpec as P

CAP = 2
SIDE = 4
BF = jnp.bfloat16
F32 = jnp.float32
VMEM = 48 * 1024 * 1024


def shifted(value, axis, shift):
    return lax.ppermute(value, axis, [(i, (i + shift) % SIDE) for i in range(SIDE)])


def params():
    return pltpu.CompilerParams(vmem_limit_bytes=VMEM)


def cost(flops, bytes_accessed):
    return pl.CostEstimate(flops=flops, bytes_accessed=bytes_accessed, transcendentals=0)


def plan_kernel(where, owner, nu, out, count):
    x, z, c = where[0], where[1], where[2]
    for o in range(16):
        count[o] = 0
    for j in range(16):
        target = owner[j, 0]
        rank = jnp.minimum(count[target], CAP - 1)
        count[target] = rank + 1
        to_x, to_z = target // 4, target % 4
        out[0, j] = to_z * 8 + to_x * 2 + rank
        out[1, j] = to_z * 2 + rank
        out[2, j] = (to_x - x + 4) % 4
        out[6, j] = nu[j] // 4
        out[7, j] = (nu[j] % 2) * 128
        out[8, j] = jnp.where((nu[j] % 4) // 2 == c, 0, 1)


def plan(where, owner, nu):
    smem = pl.BlockSpec(memory_space=pltpu.SMEM)
    return pl.pallas_call(
        plan_kernel,
        in_specs=[smem] * 3,
        out_specs=smem,
        out_shape=jax.ShapeDtypeStruct((9, 16), jnp.int32),
        scratch_shapes=[pltpu.SMEM((16,), jnp.int32)],
        name="plan",
    )(where, owner, nu)


def transform_kernel(
    meta, live, tile_hbm, mask_ref, own_hbm, other_hbm, a_hbm, b0_hbm, b1_hbm, b2_hbm, b3_hbm,
    tile, orb, result, tile_sem, orb_sem, a_sem, b_sem,
):
    def tile_copy(j):
        return pltpu.make_async_copy(tile_hbm.at[j], tile.at[j], tile_sem.at[j])

    def orb_copy(j, source):
        rows = pl.ds(pl.multiple_of(meta[7, j], 128), 128)
        return pltpu.make_async_copy(source.at[meta[6, j], rows], orb.at[j], orb_sem.at[j])

    def a_copy(j):
        return pltpu.make_async_copy(
            result.at[j, pl.ds(0, 4)], a_hbm.at[meta[0, j]], a_sem.at[j]
        )

    def b_copy(j, target):
        return pltpu.make_async_copy(
            result.at[j, pl.ds(4, 4)], target.at[meta[1, j]], b_sem.at[j]
        )

    def begin(j, carry):
        tile_copy(j).start()

        @pl.when(meta[8, j] == 0)
        def _():
            orb_copy(j, own_hbm).start()

        @pl.when(meta[8, j] != 0)
        def _():
            orb_copy(j, other_hbm).start()

        return carry

    def work(j, carry):
        tile_copy(j).wait()
        orb_copy(j, own_hbm).wait()
        masked = (tile[j] * mask_ref[j][None]).reshape(8 * 128, 128)
        product = jnp.dot(masked, orb[j], preferred_element_type=F32).astype(BF)
        result[j] = product.reshape(8, 128, 128)
        a_copy(j).start()
        for s, target in enumerate((b0_hbm, b1_hbm, b2_hbm, b3_hbm)):

            @pl.when(meta[2, j] == s)
            def _(target=target):
                b_copy(j, target).start()

        return carry

    def end(j, carry):
        a_copy(j).wait()
        b_copy(j, b0_hbm).wait()
        return carry

    lax.fori_loop(0, live[0], begin, 0)
    lax.fori_loop(0, live[0], work, 0)
    lax.fori_loop(0, live[0], end, 0)


def transform(meta, live, tiles, mask, own, other):
    smem = pl.BlockSpec(memory_space=pltpu.SMEM)
    hbm = pl.BlockSpec(memory_space=pl.ANY)
    vmem = pl.BlockSpec(memory_space=pltpu.VMEM)
    sems = pltpu.SemaphoreType.DMA((16,))
    return pl.pallas_call(
        transform_kernel,
        in_specs=[smem, smem, hbm, vmem, hbm, hbm],
        out_specs=[hbm] * 5,
        out_shape=[jax.ShapeDtypeStruct((32, 4, 128, 128), BF)]
        + [jax.ShapeDtypeStruct((8, 4, 128, 128), BF)] * 4,
        scratch_shapes=[
            pltpu.VMEM((16, 8, 128, 128), BF),
            pltpu.VMEM((16, 128, 128), BF),
            pltpu.VMEM((16, 8, 128, 128), BF),
            sems,
            sems,
            sems,
            sems,
        ],
        compiler_params=params(),
        cost_estimate=cost(2 * 16 * 8 * 128**3, 10 * 2**20),
        name="transform",
    )(meta, live, tiles, mask, own, other)


def collect_kernel(
    along_x, codes, source, place, mine, a_ref, b_ref, c_ref, d_ref, out_ref, acc, table, count
):
    j = pl.program_id(0)

    @pl.when(j == 0)
    def _():
        for k in range(SIDE):
            for t in range(SIDE):
                count[t] = 0
                for r in range(CAP):
                    table[(k * SIDE + t) * CAP + r] = 0
            row = source[k]

            def visit(slot, carry):
                code = codes[row, slot]
                owner = code // 4
                fixed, free = (owner // 4, owner % 4) if along_x else (owner % 4, owner // 4)

                @pl.when(jnp.logical_and(code >= 0, fixed == mine[0]))
                def _():
                    rank = jnp.minimum(count[free], CAP - 1)
                    table[(k * SIDE + free) * CAP + rank] = code % 4 + 1
                    count[free] = rank + 1

                return carry

            lax.fori_loop(0, 16, visit, 0)

    acc[...] = jnp.zeros(acc.shape, F32)
    for k, ref in enumerate((a_ref, b_ref, c_ref, d_ref)):
        for r in range(CAP):
            code = table[(k * SIDE + j) * CAP + r]

            @pl.when(code > 0)
            def _(ref=ref, r=r, code=code):
                acc[code - 1] += ref[0, r].astype(F32)

    for s in range(4):
        out_ref[0, :, s * 128 : (s + 1) * 128, :] = acc[s].astype(BF)


def collect(along_x, codes, source, place, mine, pieces, offsets):
    block = (1, CAP, 4, 128, 128)
    specs = [
        pl.BlockSpec(block, functools.partial(lambda o, j, *_: (o + j, 0, 0, 0, 0), o))
        for o in offsets
    ]
    grid_spec = pltpu.PrefetchScalarGridSpec(
        num_scalar_prefetch=4,
        grid=(SIDE,),
        in_specs=specs,
        out_specs=pl.BlockSpec(
            (1, 4, 512, 128), lambda j, codes, source, place, mine: (place[j], 0, 0, 0)
        ),
        scratch_shapes=[
            pltpu.VMEM((4, 4, 128, 128), F32),
            pltpu.SMEM((4 * SIDE * CAP,), jnp.int32),
            pltpu.SMEM((SIDE,), jnp.int32),
        ],
    )
    return pl.pallas_call(
        functools.partial(collect_kernel, along_x),
        grid_spec=grid_spec,
        out_shape=jax.ShapeDtypeStruct((SIDE, 4, 512, 128), BF),
        compiler_params=params(),
        cost_estimate=cost(2**22, 6 * 2**20),
        name="collect",
    )(codes, source, place, mine, *pieces)


def finish_kernel(*refs):
    out_ref = refs[-1]
    for half in range(2):
        total = refs[4 * half][0].astype(F32)
        for k in range(1, 4):
            total += refs[4 * half + k][0].astype(F32)
        for p in range(4):
            turned = total[p].T.astype(BF)
            out_ref[:, 4 * half + p] = turned.reshape(8, 16, 128)


def finish(pieces, offsets):
    specs = [
        pl.BlockSpec((1, 4, 128, 128), functools.partial(lambda o, m: (o, 0, m, 0), o))
        for o in offsets
    ]
    return pl.pallas_call(
        finish_kernel,
        grid=(4,),
        in_specs=specs,
        out_specs=pl.BlockSpec((8, 8, 16, 128), lambda m: (0, 0, 0, m)),
        out_shape=jax.ShapeDtypeStruct((8, 8, 16, 512), BF),
        compiler_params=params(),
        cost_estimate=cost(2**21, 5 * 2**20),
        name="finish",
    )(*pieces)


def product_kernel(has_add, zsel, psel, left_ref, f0, f1, f2, f3, *rest):
    out_ref = rest[-1]
    x2 = pl.program_id(0)
    for s, ref in enumerate((f0, f1, f2, f3)):

        @pl.when(psel[x2] == s)
        def _(ref=ref):
            value = jnp.dot(left_ref[0], ref[...], preferred_element_type=F32)
            if has_add:
                value += rest[0][0].astype(F32)
            out_ref[0] = value.astype(BF)


def product(zsel, psel, left, columns, add=None):
    whole = pl.BlockSpec((1024, 512), lambda x2, *_: (0, 0))
    tile = pl.BlockSpec((1, 512, 512), lambda x2, *_: (x2, 0, 0))
    specs = [pl.BlockSpec((1, 512, 1024), lambda x2, zsel, psel: (zsel[0], 0, 0))] + [whole] * 4
    operands = [left, *columns]
    if add is not None:
        specs.append(tile)
        operands.append(add)
    grid_spec = pltpu.PrefetchScalarGridSpec(
        num_scalar_prefetch=2, grid=(SIDE,), in_specs=specs, out_specs=tile
    )
    return pl.pallas_call(
        functools.partial(product_kernel, add is not None),
        grid_spec=grid_spec,
        out_shape=jax.ShapeDtypeStruct((SIDE, 512, 512), BF),
        compiler_params=params(),
        cost_estimate=cost(4 * 2 * 512 * 512 * 1024, 7 * 2**20),
        name="product",
    )(zsel, psel, *operands)


def per_device(
    three_index, pair_mask, pair_owner, pair_sub, pair_nu, live_count, coefficients, fit_matrix
):
    slots = three_index.shape[0]
    x, z, y, c = (lax.axis_index(name) for name in ("x", "z", "y", "c"))

    swapped_fit = lax.ppermute(fit_matrix, "c", [(0, 1), (1, 0)])
    pair_fit = jnp.where(
        c == 0,
        jnp.concatenate([fit_matrix, swapped_fit], 0),
        jnp.concatenate([swapped_fit, fit_matrix], 0),
    )
    fits = jnp.stack([pair_fit] + [shifted(pair_fit, "y", s) for s in (1, 2, 3)])
    fit = fits[(y - jnp.arange(4)) % 4].reshape(64, 64)

    alive = jnp.arange(slots) < live_count[0]
    code = jnp.where(alive, pair_owner[:, 0] * 4 + pair_sub, -1).astype(BF)
    half_blocks = lax.dynamic_slice_in_dim(coefficients, c * 256, 256, 0)
    code_rows = jnp.broadcast_to(jnp.pad(code, (0, 112))[None], (16, 128))
    sent = jnp.concatenate([half_blocks, code_rows], 0)
    own = lax.all_to_all(
        jnp.broadcast_to(sent[None], (16, 272, 128)), ("x", "z"), 0, 0, tiled=True
    )
    other = lax.ppermute(own, "c", [(0, 1), (1, 0)])
    codes = own[:, 256, :slots].astype(jnp.int32)

    where = jnp.stack([x, z, c]).astype(jnp.int32)
    meta = plan(where, pair_owner, pair_nu)
    mask = jnp.repeat(jnp.repeat(pair_mask, 16, 1), 16, 2).astype(BF)

    out_a, *out_b = transform(meta, live_count, three_index, mask, own, other)
    got_a = lax.all_to_all(
        out_a.reshape(4, 8, 4, 128, 128), "z", 0, 0, tiled=True
    ).reshape(16, CAP, 4, 128, 128)
    out_b = [piece.reshape(4, CAP, 4, 128, 128) for piece in out_b]
    got_b = [out_b[0]] + [shifted(out_b[s], "x", s) for s in (1, 2, 3)]
    steps = jnp.arange(4, dtype=jnp.int32)
    sum_a = collect(False, codes, x * 4 + steps, steps, z[None], [got_a] * 4, (0, 4, 8, 12))
    last_a = lax.all_to_all(sum_a, "x", 0, 0, tiled=True)
    sum_b = collect(
        True, codes, (x - steps) % 4 * 4 + z, (steps - z) % 4, x[None], got_b, (0,) * 4
    )
    last_b = [sum_b[:1]] + [shifted(sum_b[s : s + 1], "z", s) for s in (1, 2, 3)]
    cut = finish([last_a] * 4 + last_b, (0, 1, 2, 3, 0, 0, 0, 0))

    rows = lax.all_to_all(cut, ("y", "c"), 0, 0, tiled=True).reshape(1024, 512)

    spread = (jnp.arange(1024)[:, None] // 16 == jnp.arange(64)[None, :]).astype(BF)
    mixing = jnp.dot(jnp.dot(spread, fit, preferred_element_type=F32).astype(BF), spread.T)
    same = jnp.arange(1024)[:, None] % 16 == jnp.arange(1024)[None, :] % 16
    mixing = jnp.where(same, mixing, 0).astype(BF)

    fitted = jnp.dot(mixing, rows, preferred_element_type=F32).astype(BF)
    left = lax.all_to_all(
        jnp.broadcast_to(rows.T[None], (4, 512, 1024)), "z", 0, 0, tiled=True
    )
    columns = [fitted] + [shifted(fitted, "x", s) for s in (1, 2, 3)]

    psel = ((x - jnp.arange(4)) % 4).astype(jnp.int32)
    swap = [(0, 1), (1, 0)]
    turns = [((z + t) % 2)[None] for t in range(2)]
    theirs = [product(2 * (1 - c) + turn, psel, left, columns) for turn in turns]
    theirs = [lax.ppermute(part, "c", swap) for part in theirs]
    got = []
    for t in range(2):
        partial = product(2 * c + turns[t], psel, left, columns, theirs[t])
        parts = lax.all_to_all(partial, "y", 0, 0, tiled=True)
        tile = jnp.sum(parts.astype(F32), 0).astype(BF)
        pairs = [
            (zz * 2 + k, (2 * k + (zz + t) % 2) * 2 + zz // 2) for zz in range(4) for k in range(2)
        ]
        got.append(lax.ppermute(tile, ("z", "c"), pairs).astype(F32))
    scale = 8192 ** (-0.5)
    even = z % 2 == 0
    first = jnp.where(even, got[0], got[1]) * scale
    second = jnp.where(even, got[1], got[0]) * scale
    return jnp.concatenate([first, second], 1)


def solution(mesh):
    grid = Mesh(mesh.devices.reshape(4, 4, 4, 2), ("x", "z", "y", "c"))
    atom, aux = ("x", "z"), ("y", "c")
    in_specs = (
        P(atom, aux, None, None),
        P(atom, None, None),
        P(atom, None),
        P(atom),
        P(atom),
        P(atom),
        P(atom, None),
        P(aux, None),
    )
    return jax.shard_map(
        per_device, mesh=grid, in_specs=in_specs, out_specs=P(atom, aux), check_vma=False
    )
```

```python
import functools

import jax
import jax.numpy as jnp
from jax import lax
from jax.experimental import pallas as pl
from jax.experimental.pallas import tpu as pltpu
from jax.sharding import Mesh
from jax.sharding import PartitionSpec as P

CAP = 2
SIDE = 4
MAIN = 6
CHUNKS = 1
BF = jnp.bfloat16
F32 = jnp.float32
VMEM = 60 * 1024 * 1024


def shifted(value, axis, shift):
    return lax.ppermute(value, axis, [(i, (i + shift) % SIDE) for i in range(SIDE)])


def params():
    return pltpu.CompilerParams(vmem_limit_bytes=VMEM)


def cost(flops, bytes_accessed):
    return pl.CostEstimate(flops=flops, bytes_accessed=bytes_accessed, transcendentals=0)


def plan_kernel(where, owner, nu, out, count):
    x, z, c = where[0], where[1], where[2]
    for o in range(2 * SIDE):
        count[o] = 0
    for j in range(16):
        target = owner[j, 0]
        to_x, to_z = target // 4, target % 4
        out[0, j] = to_z
        out[1, j] = count[to_z]
        count[to_z] = count[to_z] + 1
        out[2, j] = (to_x - x + 4) % 4
        out[3, j] = count[SIDE + to_x]
        count[SIDE + to_x] = count[SIDE + to_x] + 1
        atom = nu[j] // 4
        half = (nu[j] % 4) // 2
        out[4, j] = (z - atom % 4 + 4) % 4 + jnp.where(half == c, 0, SIDE)
        out[5, j] = (x - atom // 4 + 4) % 4
        out[6, j] = (nu[j] % 2) * 128


def plan(where, owner, nu):
    smem = pl.BlockSpec(memory_space=pltpu.SMEM)
    return pl.pallas_call(
        plan_kernel,
        in_specs=[smem] * 3,
        out_specs=smem,
        out_shape=jax.ShapeDtypeStruct((7, 16), jnp.int32),
        scratch_shapes=[pltpu.SMEM((2 * SIDE,), jnp.int32)],
        name="plan",
    )(where, owner, nu)


def transform_kernel(first, size, meta, live, tile_hbm, mask_ref, *refs):
    orb_hbm = refs[:8]
    a_main, a_extra, b_extra = refs[8:11]
    b_main = refs[11:15]
    tile, orb, result, tile_sem, orb_sem, a_sem, b_sem = refs[15:]

    def tile_copies(j):
        return [
            pltpu.make_async_copy(
                tile_hbm.at[j, pl.ds(start, size)], tile.at[j, pl.ds(h * size, size)], tile_sem.at[h, j]
            )
            for h, start in enumerate((first, 4 + first))
        ]

    def orb_copy(j, source):
        rows = pl.ds(pl.multiple_of(meta[6, j], 128), 128)
        return pltpu.make_async_copy(source.at[meta[5, j], rows], orb.at[j], orb_sem.at[j])

    def a_copy(j, target):
        return pltpu.make_async_copy(result.at[j, pl.ds(0, size)], target, a_sem.at[j])

    def b_copy(j, target):
        return pltpu.make_async_copy(result.at[j, pl.ds(size, size)], target, b_sem.at[j])

    def begin(j, carry):
        for copy in tile_copies(j):
            copy.start()
        for k, source in enumerate(orb_hbm):

            @pl.when(meta[4, j] == k)
            def _(source=source):
                orb_copy(j, source).start()

        return carry

    def work(j, carry):
        for copy in tile_copies(j):
            copy.wait()
        orb_copy(j, orb_hbm[0]).wait()
        masked = (tile[j] * mask_ref[j][None]).reshape(2 * size * 128, 128)
        product = jnp.dot(masked, orb[j], preferred_element_type=F32).astype(BF)
        result[j] = product.reshape(2 * size, 128, 128)
        group, entry = meta[0, j], meta[1, j]

        @pl.when(entry < MAIN)
        def _():
            a_copy(j, a_main.at[group, entry]).start()

        @pl.when(entry >= MAIN)
        def _():
            a_copy(j, a_extra.at[group, entry - MAIN]).start()

        piece, place = meta[2, j], meta[3, j]
        for s, target in enumerate(b_main):

            @pl.when(jnp.logical_and(piece == s, place < MAIN))
            def _(target=target):
                b_copy(j, target.at[place]).start()

        @pl.when(place >= MAIN)
        def _():
            b_copy(j, b_extra.at[piece, place - MAIN]).start()

        return carry

    def end(j, carry):
        a_copy(j, a_main.at[0, 0]).wait()
        b_copy(j, b_main[0].at[0]).wait()
        return carry

    lax.fori_loop(0, live[0], begin, 0)
    lax.fori_loop(0, live[0], work, 0)
    lax.fori_loop(0, live[0], end, 0)


def transform(first, size, meta, live, tiles, mask, orbitals):
    smem = pl.BlockSpec(memory_space=pltpu.SMEM)
    hbm = pl.BlockSpec(memory_space=pltpu.HBM)
    vmem = pl.BlockSpec(memory_space=pltpu.VMEM)
    sems = pltpu.SemaphoreType.DMA((16,))
    shapes = [(4, MAIN), (4, 8 - MAIN), (4, 8 - MAIN)] + [(MAIN,)] * 4
    return pl.pallas_call(
        functools.partial(transform_kernel, first, size),
        in_specs=[smem, smem, hbm, vmem] + [hbm] * 8,
        out_specs=[hbm] * 7,
        out_shape=[jax.ShapeDtypeStruct(shape + (size, 128, 128), BF) for shape in shapes],
        scratch_shapes=[
            pltpu.VMEM((16, 2 * size, 128, 128), BF),
            pltpu.VMEM((16, 128, 128), BF),
            pltpu.VMEM((16, 2 * size, 128, 128), BF),
            pltpu.SemaphoreType.DMA((2, 16)),
            sems,
            sems,
            sems,
        ],
        compiler_params=params(),
        cost_estimate=cost(2 * 16 * 2 * size * 128**3, 16 * 2 * size * 2**16),
        name="transform",
    )(meta, live, tiles, mask, *orbitals)


def collect_kernel(along_x, size, codes, source, place, mine, *refs):
    if along_x:
        main, extra, outs, rest = refs[:4], refs[4], refs[5:9], refs[9:]
    else:
        main, extra, outs, rest = [refs[0].at[k] for k in range(4)], refs[1], refs[2:3], refs[3:]
    buffer, acc, result, table, count, in_sem, out_sem = rest

    def arrival(k, q, origin):
        return pltpu.make_async_copy(origin, buffer.at[k, q], in_sem.at[k, q])

    def departure(j, target):
        return pltpu.make_async_copy(result.at[j], target, out_sem.at[j])

    for k in range(SIDE):
        for t in range(SIDE):
            count[t] = 0
            for r in range(CAP):
                table[(k * SIDE + t) * CAP + r] = 0
        row = source[k]

        def visit(slot, q, k=k, row=row):
            code = codes[row, slot]
            owner = code // 4
            fixed, free = (owner // 4, owner % 4) if along_x else (owner % 4, owner // 4)
            hit = jnp.logical_and(code >= 0, fixed == mine[0])

            @pl.when(hit)
            def _():
                rank = jnp.minimum(count[free], CAP - 1)
                table[(k * SIDE + free) * CAP + rank] = q * 4 + code % 4 + 1
                count[free] = rank + 1

            @pl.when(jnp.logical_and(hit, q < MAIN))
            def _():
                arrival(k, q, main[k].at[q]).start()

            @pl.when(jnp.logical_and(hit, q >= MAIN))
            def _():
                arrival(k, q, extra.at[k, q - MAIN]).start()

            return q + hit.astype(jnp.int32)

        lax.fori_loop(0, 16, visit, jnp.int32(0))

    for j in range(SIDE):
        acc[...] = jnp.zeros(acc.shape, F32)
        for k in range(SIDE):
            for r in range(CAP):
                code = table[(k * SIDE + j) * CAP + r]

                @pl.when(code > 0)
                def _(k=k, code=code):
                    q, sub = (code - 1) // 4, (code - 1) % 4
                    arrival(k, q, main[k].at[0]).wait()
                    acc[sub] += buffer[k, q].astype(F32)

        for s in range(4):
            result[j, :, s * 128 : (s + 1) * 128, :] = acc[s].astype(BF)
        if along_x:
            for s in range(SIDE):

                @pl.when(place[j] == s)
                def _(s=s, j=j):
                    departure(j, outs[s]).start()

        else:
            departure(j, outs[0].at[j]).start()
    for j in range(SIDE):
        departure(j, outs[0] if along_x else outs[0].at[0]).wait()


def collect(along_x, size, codes, source, place, mine, main, extra):
    smem = pl.BlockSpec(memory_space=pltpu.SMEM)
    hbm = pl.BlockSpec(memory_space=pltpu.HBM)
    out = (size, 512, 128)
    shapes = [jax.ShapeDtypeStruct(out, BF)] * 4 if along_x else [jax.ShapeDtypeStruct((4,) + out, BF)]
    return pl.pallas_call(
        functools.partial(collect_kernel, along_x, size),
        in_specs=[smem] * 4 + [hbm] * (len(main) + 1),
        out_specs=[hbm] * len(shapes),
        out_shape=shapes,
        scratch_shapes=[
            pltpu.VMEM((SIDE, 8, size, 128, 128), BF),
            pltpu.VMEM((4, size, 128, 128), F32),
            pltpu.VMEM((SIDE,) + out, BF),
            pltpu.SMEM((4 * SIDE * CAP,), jnp.int32),
            pltpu.SMEM((SIDE,), jnp.int32),
            pltpu.SemaphoreType.DMA((SIDE, 8)),
            pltpu.SemaphoreType.DMA((SIDE,)),
        ],
        compiler_params=params(),
        cost_estimate=cost(2**22, size * 3 * 2**19),
        name="collect",
    )(codes, source, place, mine, *main, extra)


def finish_kernel(size, first_ref, *refs):
    out_ref = refs[-1]
    for half in range(2):
        pieces = [first_ref[k] for k in range(4)] if half == 0 else [ref[...] for ref in refs[:4]]
        total = pieces[0].astype(F32)
        for piece in pieces[1:]:
            total += piece.astype(F32)
        for p in range(size):
            turned = total[p].T.astype(BF)
            out_ref[:, size * half + p] = turned.reshape(8, 16, 128)


def finish(size, first, pieces):
    return pl.pallas_call(
        functools.partial(finish_kernel, size),
        grid=(4,),
        in_specs=[pl.BlockSpec((4, size, 128, 128), lambda m: (0, 0, m, 0))]
        + [pl.BlockSpec((size, 128, 128), lambda m: (0, m, 0))] * 4,
        out_specs=pl.BlockSpec((8, 2 * size, 16, 128), lambda m: (0, 0, 0, m)),
        out_shape=jax.ShapeDtypeStruct((8, 2 * size, 16, 512), BF),
        compiler_params=params(),
        cost_estimate=cost(2**21, 5 * 2**20),
        name="finish",
    )(first, *pieces)


def product_kernel(has_add, zsel, psel, left_ref, f0, f1, f2, f3, *rest):
    out_ref = rest[-1]
    x2 = pl.program_id(0)
    for s, ref in enumerate((f0, f1, f2, f3)):

        @pl.when(psel[x2] == s)
        def _(ref=ref):
            value = jnp.dot(left_ref[0], ref[...], preferred_element_type=F32)
            if has_add:
                value += rest[0][0].astype(F32)
            out_ref[0] = value.astype(BF)


def product(zsel, psel, left, columns, add=None):
    whole = pl.BlockSpec((1024, 512), lambda x2, *_: (0, 0))
    tile = pl.BlockSpec((1, 512, 512), lambda x2, *_: (x2, 0, 0))
    specs = [pl.BlockSpec((1, 512, 1024), lambda x2, zsel, psel: (zsel[0], 0, 0))] + [whole] * 4
    operands = [left, *columns]
    if add is not None:
        specs.append(tile)
        operands.append(add)
    grid_spec = pltpu.PrefetchScalarGridSpec(
        num_scalar_prefetch=2, grid=(SIDE,), in_specs=specs, out_specs=tile
    )
    return pl.pallas_call(
        functools.partial(product_kernel, add is not None),
        grid_spec=grid_spec,
        out_shape=jax.ShapeDtypeStruct((SIDE, 512, 512), BF),
        compiler_params=params(),
        cost_estimate=cost(4 * 2 * 512 * 512 * 1024, 7 * 2**20),
        name="product",
    )(zsel, psel, *operands)


def per_device(
    three_index, pair_mask, pair_owner, pair_sub, pair_nu, live_count, coefficients, fit_matrix
):
    slots = three_index.shape[0]
    x, z, y, c = (lax.axis_index(name) for name in ("x", "z", "y", "c"))

    swapped_fit = lax.ppermute(fit_matrix, "c", [(0, 1), (1, 0)])
    pair_fit = jnp.where(
        c == 0,
        jnp.concatenate([fit_matrix, swapped_fit], 0),
        jnp.concatenate([swapped_fit, fit_matrix], 0),
    )
    fits = jnp.stack([pair_fit] + [shifted(pair_fit, "y", s) for s in (1, 2, 3)])
    fit = fits[(y - jnp.arange(4)) % 4].reshape(64, 64)

    alive = jnp.arange(slots) < live_count[0]
    code = jnp.where(alive, pair_owner[:, 0] * 4 + pair_sub, -1).astype(BF)
    half_blocks = lax.dynamic_slice_in_dim(coefficients, c * 256, 256, 0)
    code_rows = jnp.broadcast_to(jnp.pad(code, (0, 112))[None], (16, 128))
    sent = jnp.concatenate([half_blocks, code_rows], 0)
    swap = [(0, 1), (1, 0)]
    line = jnp.stack([sent] + [shifted(sent, "x", s) for s in (1, 2, 3)])
    halves = [line] + [shifted(line, "z", s) for s in (1, 2, 3)]
    orbitals = halves + [lax.ppermute(half, "c", swap) for half in halves]
    codes = jnp.concatenate([half[:, 256, :slots] for half in halves], 0).astype(jnp.int32)

    where = jnp.stack([x, z, c]).astype(jnp.int32)
    meta = plan(where, pair_owner, pair_nu)
    mask = jnp.repeat(jnp.repeat(pair_mask, 16, 1), 16, 2).astype(BF)
    mask, fit, meta = lax.optimization_barrier((mask, fit, meta))

    steps = jnp.arange(4, dtype=jnp.int32)
    to_x, to_z = codes // 16, codes // 4 % 4
    from_x, from_z = jnp.tile((x - steps) % 4, 4), jnp.repeat((z - steps) % 4, 4)

    def lengths(to, origin):
        hits = (codes[..., None] >= 0) & (to[..., None] == steps) & (to != origin[:, None])[..., None]
        return jnp.max(jnp.sum(hits.astype(jnp.int32), 1))

    overflow = jnp.maximum(lengths(to_x, from_x), lengths(to_z, from_z)) > MAIN

    size = 4 // CHUNKS

    def route(chunk):
        a_main, a_extra, b_extra, *b_main = transform(
            chunk * size, size, meta, live_count, three_index, mask, orbitals
        )
        a_got = lax.all_to_all(a_main, "z", 0, 0, tiled=True)
        b_got = [b_main[0]] + [shifted(b_main[s], "x", s) for s in (1, 2, 3)]

        def send_extra(a, b):
            moved = [b[:1]] + [shifted(b[s : s + 1], "x", s) for s in (1, 2, 3)]
            return lax.all_to_all(a, "z", 0, 0, tiled=True), jnp.concatenate(moved, 0)

        a_extra, b_extra = lax.cond(
            overflow, send_extra, lambda a, b: (a, b), a_extra, b_extra
        )
        (a_sum,) = collect(
            False, size, codes, (z - steps) % 4 * 4, steps, z[None], [a_got], a_extra
        )
        a_last = lax.all_to_all(a_sum, "x", 0, 0, tiled=True)
        b_sum = collect(True, size, codes, steps, (steps - z) % 4, x[None], b_got, b_extra)
        b_last = [b_sum[0]] + [shifted(b_sum[s], "z", s) for s in (1, 2, 3)]
        cut = finish(size, a_last, b_last)
        return lax.all_to_all(cut, ("y", "c"), 0, 0, tiled=True).reshape(-1, 512)

    (rows,) = [route(chunk) for chunk in range(CHUNKS)]

    spread = (jnp.arange(1024)[:, None] // 16 == jnp.arange(64)[None, :]).astype(BF)
    mixing = jnp.dot(jnp.dot(spread, fit, preferred_element_type=F32).astype(BF), spread.T)
    same = jnp.arange(1024)[:, None] % 16 == jnp.arange(1024)[None, :] % 16
    mixing = jnp.where(same, mixing, 0).astype(BF)

    fitted = jnp.dot(mixing, rows, preferred_element_type=F32).astype(BF)
    columns = [fitted] + [shifted(fitted, "x", s) for s in (1, 2, 3)]
    left = lax.all_to_all(
        jnp.broadcast_to(rows.T[None], (4, 512, 1024)), "z", 0, 0, tiled=True
    )

    psel = ((x - jnp.arange(4)) % 4).astype(jnp.int32)
    turns = [((z + t) % 2)[None] for t in range(2)]
    theirs = [product(2 * (1 - c) + turn, psel, left, columns) for turn in turns]
    theirs = [lax.ppermute(part, "c", swap) for part in theirs]
    got = []
    for t in range(2):
        partial = product(2 * c + turns[t], psel, left, columns, theirs[t])
        parts = lax.all_to_all(partial, "y", 0, 0, tiled=True)
        tile = jnp.sum(parts.astype(F32), 0).astype(BF)
        pairs = [
            (zz * 2 + k, (2 * k + (zz + t) % 2) * 2 + zz // 2) for zz in range(4) for k in range(2)
        ]
        got.append(lax.ppermute(tile, ("z", "c"), pairs).astype(F32))
    scale = 8192 ** (-0.5)
    even = z % 2 == 0
    first = jnp.where(even, got[0], got[1]) * scale
    second = jnp.where(even, got[1], got[0]) * scale
    return jnp.concatenate([first, second], 1)


def solution(mesh):
    grid = Mesh(mesh.devices.reshape(4, 4, 4, 2), ("x", "z", "y", "c"))
    atom, aux = ("x", "z"), ("y", "c")
    in_specs = (
        P(atom, aux, None, None),
        P(atom, None, None),
        P(atom, None),
        P(atom),
        P(atom),
        P(atom),
        P(atom, None),
        P(aux, None),
    )
    return jax.shard_map(
        per_device, mesh=grid, in_specs=in_specs, out_specs=P(atom, aux), check_vma=False
    )
```

```python
import functools

import jax
import jax.numpy as jnp
from jax import lax
from jax.experimental import pallas as pl
from jax.experimental.pallas import tpu as pltpu
from jax.sharding import Mesh
from jax.sharding import PartitionSpec as P

CAP = 2
SIDE = 4
MAIN = 6
CHUNKS = 1
BF = jnp.bfloat16
F32 = jnp.float32
VMEM = 40 * 1024 * 1024
MOST = 58 * 1024 * 1024


def shifted(value, axis, shift):
    return lax.ppermute(value, axis, [(i, (i + shift) % SIDE) for i in range(SIDE)])


def params(limit=VMEM):
    return pltpu.CompilerParams(vmem_limit_bytes=limit)


def cost(flops, bytes_accessed):
    return pl.CostEstimate(flops=flops, bytes_accessed=bytes_accessed, transcendentals=0)


def plan_kernel(where, owner, nu, out, count):
    x, z, c = where[0], where[1], where[2]
    for o in range(2 * SIDE):
        count[o] = 0
    for j in range(16):
        target = owner[j, 0]
        to_x, to_z = target // 4, target % 4
        out[0, j] = to_z
        out[1, j] = count[to_z]
        count[to_z] = count[to_z] + 1
        out[2, j] = (to_x - x + 4) % 4
        out[3, j] = count[SIDE + to_x]
        count[SIDE + to_x] = count[SIDE + to_x] + 1
        atom = nu[j] // 4
        half = (nu[j] % 4) // 2
        out[4, j] = jnp.where(half == c, 0, 1)
        out[5, j] = atom
        out[6, j] = (nu[j] % 2) * 128


def plan(where, owner, nu):
    smem = pl.BlockSpec(memory_space=pltpu.SMEM)
    return pl.pallas_call(
        plan_kernel,
        in_specs=[smem] * 3,
        out_specs=smem,
        out_shape=jax.ShapeDtypeStruct((7, 16), jnp.int32),
        scratch_shapes=[pltpu.SMEM((2 * SIDE,), jnp.int32)],
        name="plan",
    )(where, owner, nu)


def transform_kernel(first, size, meta, live, tile_hbm, mask_ref, *refs):
    orb_hbm = refs[:2]
    a_main, a_extra, b_extra = refs[2:5]
    b_main = refs[5:9]
    tile, orb, result, tile_sem, orb_sem, a_sem, b_sem = refs[9:]

    def tile_copies(j):
        return [
            pltpu.make_async_copy(
                tile_hbm.at[j, pl.ds(start, size)], tile.at[j, pl.ds(h * size, size)], tile_sem.at[h, j]
            )
            for h, start in enumerate((first, 4 + first))
        ]

    def orb_copy(j, source):
        rows = pl.ds(pl.multiple_of(meta[6, j], 128), 128)
        return pltpu.make_async_copy(source.at[meta[5, j], rows], orb.at[j], orb_sem.at[j])

    def a_copy(j, target):
        return pltpu.make_async_copy(result.at[j, pl.ds(0, size)], target, a_sem.at[j])

    def b_copy(j, target):
        return pltpu.make_async_copy(result.at[j, pl.ds(size, size)], target, b_sem.at[j])

    def begin(j, carry):
        for copy in tile_copies(j):
            copy.start()
        for k, source in enumerate(orb_hbm):

            @pl.when(meta[4, j] == k)
            def _(source=source):
                orb_copy(j, source).start()

        return carry

    def work(j, carry):
        for copy in tile_copies(j):
            copy.wait()
        orb_copy(j, orb_hbm[0]).wait()
        masked = (tile[j] * mask_ref[j][None]).reshape(2 * size * 128, 128)
        product = jnp.dot(masked, orb[j], preferred_element_type=F32).astype(BF)
        result[j] = product.reshape(2 * size, 128, 128)
        group, entry = meta[0, j], meta[1, j]

        @pl.when(entry < MAIN)
        def _():
            a_copy(j, a_main.at[group, entry]).start()

        @pl.when(entry >= MAIN)
        def _():
            a_copy(j, a_extra.at[group, entry - MAIN]).start()

        piece, place = meta[2, j], meta[3, j]
        for s, target in enumerate(b_main):

            @pl.when(jnp.logical_and(piece == s, place < MAIN))
            def _(target=target):
                b_copy(j, target.at[place]).start()

        @pl.when(place >= MAIN)
        def _():
            b_copy(j, b_extra.at[piece, place - MAIN]).start()

        return carry

    def end(j, carry):
        a_copy(j, a_main.at[0, 0]).wait()
        b_copy(j, b_main[0].at[0]).wait()
        return carry

    lax.fori_loop(0, live[0], begin, 0)
    lax.fori_loop(0, live[0], work, 0)
    lax.fori_loop(0, live[0], end, 0)


def transform(first, size, meta, live, tiles, mask, orbitals):
    smem = pl.BlockSpec(memory_space=pltpu.SMEM)
    hbm = pl.BlockSpec(memory_space=pltpu.HBM)
    anywhere = pl.BlockSpec(memory_space=pl.ANY)
    vmem = pl.BlockSpec(memory_space=pltpu.VMEM)
    sems = pltpu.SemaphoreType.DMA((16,))
    shapes = [(4, MAIN), (4, 8 - MAIN), (4, 8 - MAIN)] + [(MAIN,)] * 4
    return pl.pallas_call(
        functools.partial(transform_kernel, first, size),
        in_specs=[smem, smem, hbm, vmem] + [anywhere] * 2,
        out_specs=[hbm] * 7,
        out_shape=[jax.ShapeDtypeStruct(shape + (size, 128, 128), BF) for shape in shapes],
        scratch_shapes=[
            pltpu.VMEM((16, 2 * size, 128, 128), BF),
            pltpu.VMEM((16, 128, 128), BF),
            pltpu.VMEM((16, 2 * size, 128, 128), BF),
            pltpu.SemaphoreType.DMA((2, 16)),
            sems,
            sems,
            sems,
        ],
        compiler_params=params(MOST),
        cost_estimate=cost(2 * 16 * 2 * size * 128**3, 16 * 2 * size * 2**16),
        name="transform",
    )(meta, live, tiles, mask, *orbitals)


def collect_kernel(along_x, size, codes, source, place, mine, *refs):
    if along_x:
        main, extra, outs, rest = refs[:4], refs[4], refs[5:9], refs[9:]
    else:
        main, extra, outs, rest = [refs[0].at[k] for k in range(4)], refs[1], refs[2:3], refs[3:]
    buffer, acc, result, table, count, in_sem, out_sem = rest

    def arrival(k, q, origin):
        return pltpu.make_async_copy(origin, buffer.at[k, q], in_sem.at[k, q])

    def departure(j, target):
        return pltpu.make_async_copy(result.at[j], target, out_sem.at[j])

    for k in range(SIDE):
        for t in range(SIDE):
            count[t] = 0
            for r in range(CAP):
                table[(k * SIDE + t) * CAP + r] = 0
        row = source[k]

        def visit(slot, q, k=k, row=row):
            code = codes[row, slot]
            owner = code // 4
            fixed, free = (owner // 4, owner % 4) if along_x else (owner % 4, owner // 4)
            hit = jnp.logical_and(code >= 0, fixed == mine[0])

            @pl.when(hit)
            def _():
                rank = jnp.minimum(count[free], CAP - 1)
                table[(k * SIDE + free) * CAP + rank] = q * 4 + code % 4 + 1
                count[free] = rank + 1

            @pl.when(jnp.logical_and(hit, q < MAIN))
            def _():
                arrival(k, q, main[k].at[q]).start()

            @pl.when(jnp.logical_and(hit, q >= MAIN))
            def _():
                arrival(k, q, extra.at[k, q - MAIN]).start()

            return q + hit.astype(jnp.int32)

        lax.fori_loop(0, 16, visit, jnp.int32(0))

    for j in range(SIDE):
        acc[...] = jnp.zeros(acc.shape, F32)
        for k in range(SIDE):
            for r in range(CAP):
                code = table[(k * SIDE + j) * CAP + r]

                @pl.when(code > 0)
                def _(k=k, code=code):
                    q, sub = (code - 1) // 4, (code - 1) % 4
                    arrival(k, q, main[k].at[0]).wait()
                    acc[sub] += buffer[k, q].astype(F32)

        for s in range(4):
            result[j, :, s * 128 : (s + 1) * 128, :] = acc[s].astype(BF)
        if along_x:
            for s in range(SIDE):

                @pl.when(place[j] == s)
                def _(s=s, j=j):
                    departure(j, outs[s]).start()

        else:
            departure(j, outs[0].at[j]).start()
    for j in range(SIDE):
        departure(j, outs[0] if along_x else outs[0].at[0]).wait()


def collect(along_x, size, codes, source, place, mine, main, extra):
    smem = pl.BlockSpec(memory_space=pltpu.SMEM)
    hbm = pl.BlockSpec(memory_space=pltpu.HBM)
    anywhere = pl.BlockSpec(memory_space=pl.ANY)
    out = (size, 512, 128)
    shapes = [jax.ShapeDtypeStruct(out, BF)] * 4 if along_x else [jax.ShapeDtypeStruct((4,) + out, BF)]
    return pl.pallas_call(
        functools.partial(collect_kernel, along_x, size),
        in_specs=[smem] * 4 + [anywhere] * (len(main) + 1),
        out_specs=[hbm] * len(shapes),
        out_shape=shapes,
        scratch_shapes=[
            pltpu.VMEM((SIDE, 8, size, 128, 128), BF),
            pltpu.VMEM((4, size, 128, 128), F32),
            pltpu.VMEM((SIDE,) + out, BF),
            pltpu.SMEM((4 * SIDE * CAP,), jnp.int32),
            pltpu.SMEM((SIDE,), jnp.int32),
            pltpu.SemaphoreType.DMA((SIDE, 8)),
            pltpu.SemaphoreType.DMA((SIDE,)),
        ],
        compiler_params=params(MOST),
        cost_estimate=cost(2**22, size * 3 * 2**19),
        name="collect",
    )(codes, source, place, mine, *main, extra)


def finish_kernel(size, first_ref, *refs):
    out_ref = refs[-1]
    for half in range(2):
        pieces = [first_ref[k] for k in range(4)] if half == 0 else [ref[...] for ref in refs[:4]]
        total = pieces[0].astype(F32)
        for piece in pieces[1:]:
            total += piece.astype(F32)
        for p in range(size):
            turned = total[p].T.astype(BF)
            out_ref[:, size * half + p] = turned.reshape(8, 16, 128)


def finish(size, first, pieces):
    return pl.pallas_call(
        functools.partial(finish_kernel, size),
        grid=(4,),
        in_specs=[pl.BlockSpec((4, size, 128, 128), lambda m: (0, 0, m, 0))]
        + [pl.BlockSpec((size, 128, 128), lambda m: (0, m, 0))] * 4,
        out_specs=pl.BlockSpec((8, 2 * size, 16, 128), lambda m: (0, 0, 0, m)),
        out_shape=jax.ShapeDtypeStruct((8, 2 * size, 16, 512), BF),
        compiler_params=params(),
        cost_estimate=cost(2**21, 5 * 2**20),
        name="finish",
    )(first, *pieces)


def product_kernel(has_add, zsel, psel, left_ref, f0, f1, f2, f3, *rest):
    out_ref = rest[-1]
    x2 = pl.program_id(0)
    for s, ref in enumerate((f0, f1, f2, f3)):

        @pl.when(psel[x2] == s)
        def _(ref=ref):
            value = jnp.dot(left_ref[0], ref[...], preferred_element_type=F32)
            if has_add:
                value += rest[0][0].astype(F32)
            out_ref[0] = value.astype(BF)


def product(zsel, psel, left, columns, add=None):
    whole = pl.BlockSpec((1024, 512), lambda x2, *_: (0, 0))
    tile = pl.BlockSpec((1, 512, 512), lambda x2, *_: (x2, 0, 0))
    specs = [pl.BlockSpec((1, 512, 1024), lambda x2, zsel, psel: (zsel[0], 0, 0))] + [whole] * 4
    operands = [left, *columns]
    if add is not None:
        specs.append(tile)
        operands.append(add)
    grid_spec = pltpu.PrefetchScalarGridSpec(
        num_scalar_prefetch=2, grid=(SIDE,), in_specs=specs, out_specs=tile
    )
    return pl.pallas_call(
        functools.partial(product_kernel, add is not None),
        grid_spec=grid_spec,
        out_shape=jax.ShapeDtypeStruct((SIDE, 512, 512), BF),
        compiler_params=params(),
        cost_estimate=cost(4 * 2 * 512 * 512 * 1024, 7 * 2**20),
        name="product",
    )(zsel, psel, *operands)


def per_device(
    three_index, pair_mask, pair_owner, pair_sub, pair_nu, live_count, coefficients, fit_matrix
):
    slots = three_index.shape[0]
    x, z, y, c = (lax.axis_index(name) for name in ("x", "z", "y", "c"))

    swapped_fit = lax.ppermute(fit_matrix, "c", [(0, 1), (1, 0)])
    pair_fit = jnp.where(
        c == 0,
        jnp.concatenate([fit_matrix, swapped_fit], 0),
        jnp.concatenate([swapped_fit, fit_matrix], 0),
    )
    fits = jnp.stack([pair_fit] + [shifted(pair_fit, "y", s) for s in (1, 2, 3)])
    fit = fits[(y - jnp.arange(4)) % 4].reshape(64, 64)

    alive = jnp.arange(slots) < live_count[0]
    code = jnp.where(alive, pair_owner[:, 0] * 4 + pair_sub, -1).astype(BF)
    half_blocks = lax.dynamic_slice_in_dim(coefficients, c * 256, 256, 0)
    code_rows = jnp.broadcast_to(jnp.pad(code, (0, 112))[None], (16, 128))
    sent = jnp.concatenate([half_blocks, code_rows], 0)
    swap = [(0, 1), (1, 0)]
    own = lax.all_to_all(
        jnp.broadcast_to(sent[None], (16, 272, 128)), ("x", "z"), 0, 0, tiled=True
    )

    where = jnp.stack([x, z, c]).astype(jnp.int32)
    meta = plan(where, pair_owner, pair_nu)
    mask = jnp.repeat(jnp.repeat(pair_mask, 16, 1), 16, 2).astype(BF)
    own, mask, fit, meta = lax.optimization_barrier((own, mask, fit, meta))
    orbitals = [own, lax.ppermute(own, "c", swap)]
    codes = own[:, 256, :slots].astype(jnp.int32)

    steps = jnp.arange(4, dtype=jnp.int32)
    to_x, to_z = codes // 16, codes // 4 % 4
    from_x, from_z = jnp.repeat(steps, 4), jnp.tile(steps, 4)

    def lengths(to, origin):
        hits = (codes[..., None] >= 0) & (to[..., None] == steps) & (to != origin[:, None])[..., None]
        return jnp.max(jnp.sum(hits.astype(jnp.int32), 1))

    overflow = jnp.maximum(lengths(to_x, from_x), lengths(to_z, from_z)) > MAIN

    size = 4 // CHUNKS

    def route(chunk):
        a_main, a_extra, b_extra, *b_main = transform(
            chunk * size, size, meta, live_count, three_index, mask, orbitals
        )
        a_got = lax.all_to_all(a_main, "z", 0, 0, tiled=True)
        b_got = [b_main[0]] + [shifted(b_main[s], "x", s) for s in (1, 2, 3)]
        a_got, *b_got = lax.optimization_barrier((a_got, *b_got))

        def send_extra(a, b):
            moved = [b[:1]] + [shifted(b[s : s + 1], "x", s) for s in (1, 2, 3)]
            return lax.all_to_all(a, "z", 0, 0, tiled=True), jnp.concatenate(moved, 0)

        a_extra, b_extra = lax.cond(
            overflow, send_extra, lambda a, b: (a, b), a_extra, b_extra
        )
        (a_sum,) = collect(
            False, size, codes, x * 4 + steps, steps, z[None], [a_got], a_extra
        )
        a_last = lax.all_to_all(a_sum, "x", 0, 0, tiled=True)
        b_sum = collect(
            True, size, codes, (x - steps) % 4 * 4 + z, (steps - z) % 4, x[None], b_got, b_extra
        )
        b_last = [b_sum[0]] + [shifted(b_sum[s], "z", s) for s in (1, 2, 3)]
        cut = finish(size, a_last, b_last)
        return lax.all_to_all(cut, ("y", "c"), 0, 0, tiled=True).reshape(-1, 512)

    (rows,) = [route(chunk) for chunk in range(CHUNKS)]

    spread = (jnp.arange(1024)[:, None] // 16 == jnp.arange(64)[None, :]).astype(BF)
    mixing = jnp.dot(jnp.dot(spread, fit, preferred_element_type=F32).astype(BF), spread.T)
    same = jnp.arange(1024)[:, None] % 16 == jnp.arange(1024)[None, :] % 16
    mixing = jnp.where(same, mixing, 0).astype(BF)

    fitted = jnp.dot(mixing, rows, preferred_element_type=F32).astype(BF)
    columns = [fitted] + [shifted(fitted, "x", s) for s in (1, 2, 3)]
    left = lax.all_to_all(
        jnp.broadcast_to(rows.T[None], (4, 512, 1024)), "z", 0, 0, tiled=True
    )

    psel = ((x - jnp.arange(4)) % 4).astype(jnp.int32)
    turns = [((z + t) % 2)[None] for t in range(2)]
    theirs = [product(2 * (1 - c) + turn, psel, left, columns) for turn in turns]
    theirs = [lax.ppermute(part, "c", swap) for part in theirs]
    got = []
    for t in range(2):
        partial = product(2 * c + turns[t], psel, left, columns, theirs[t])
        parts = lax.all_to_all(partial, "y", 0, 0, tiled=True)
        tile = jnp.sum(parts.astype(F32), 0).astype(BF)
        pairs = [
            (zz * 2 + k, (2 * k + (zz + t) % 2) * 2 + zz // 2) for zz in range(4) for k in range(2)
        ]
        got.append(lax.ppermute(tile, ("z", "c"), pairs).astype(F32))
    scale = 8192 ** (-0.5)
    even = z % 2 == 0
    first = jnp.where(even, got[0], got[1]) * scale
    second = jnp.where(even, got[1], got[0]) * scale
    return jnp.concatenate([first, second], 1)


def solution(mesh):
    grid = Mesh(mesh.devices.reshape(4, 4, 4, 2), ("x", "z", "y", "c"))
    atom, aux = ("x", "z"), ("y", "c")
    in_specs = (
        P(atom, aux, None, None),
        P(atom, None, None),
        P(atom, None),
        P(atom),
        P(atom),
        P(atom),
        P(atom, None),
        P(aux, None),
    )
    return jax.shard_map(
        per_device, mesh=grid, in_specs=in_specs, out_specs=P(atom, aux), check_vma=False
    )
```

```python
import functools

import jax
import jax.numpy as jnp
from jax import lax
from jax.experimental import pallas as pl
from jax.experimental.pallas import tpu as pltpu
from jax.sharding import Mesh
from jax.sharding import PartitionSpec as P

CAP = 2
SIDE = 4
MAIN = 6
BF = jnp.bfloat16
F32 = jnp.float32
VMEM = 40 * 1024 * 1024
MOST = 58 * 1024 * 1024


def shifted(value, axis, shift):
    return lax.ppermute(value, axis, [(i, (i + shift) % SIDE) for i in range(SIDE)])


def params(limit=VMEM):
    return pltpu.CompilerParams(vmem_limit_bytes=limit)


def cost(flops, bytes_accessed):
    return pl.CostEstimate(flops=flops, bytes_accessed=bytes_accessed, transcendentals=0)


def plan_kernel(where, owner, nu, out, count):
    x, z, c = where[0], where[1], where[2]
    for o in range(2 * SIDE):
        count[o] = 0
    for j in range(16):
        target = owner[j, 0]
        to_x, to_z = target // 4, target % 4
        out[0, j] = to_z
        out[1, j] = count[to_z]
        count[to_z] = count[to_z] + 1
        out[2, j] = (to_x - x + 4) % 4
        out[3, j] = count[SIDE + to_x]
        count[SIDE + to_x] = count[SIDE + to_x] + 1
        atom = nu[j] // 4
        half = (nu[j] % 4) // 2
        out[4, j] = jnp.where(half == c, 0, 1)
        out[5, j] = atom
        out[6, j] = (nu[j] % 2) * 128


def plan(where, owner, nu):
    smem = pl.BlockSpec(memory_space=pltpu.SMEM)
    return pl.pallas_call(
        plan_kernel,
        in_specs=[smem] * 3,
        out_specs=smem,
        out_shape=jax.ShapeDtypeStruct((7, 16), jnp.int32),
        scratch_shapes=[pltpu.SMEM((2 * SIDE,), jnp.int32)],
        name="plan",
    )(where, owner, nu)


def transform_kernel(first, size, meta, live, tile_hbm, mask_ref, *refs):
    orb_hbm = refs[:2]
    a_main, a_extra, b_extra = refs[2:5]
    b_main = refs[5:9]
    tile, orb, result, tile_sem, orb_sem, a_sem, b_sem = refs[9:]

    def tile_copies(j):
        return [
            pltpu.make_async_copy(
                tile_hbm.at[j, pl.ds(start, size)], tile.at[j, pl.ds(h * size, size)], tile_sem.at[h, j]
            )
            for h, start in enumerate((first, 4 + first))
        ]

    def orb_copy(j, source):
        rows = pl.ds(pl.multiple_of(meta[6, j], 128), 128)
        return pltpu.make_async_copy(source.at[meta[5, j], rows], orb.at[j], orb_sem.at[j])

    def a_copy(j, target):
        return pltpu.make_async_copy(result.at[j, pl.ds(0, size)], target, a_sem.at[j])

    def b_copy(j, target):
        return pltpu.make_async_copy(result.at[j, pl.ds(size, size)], target, b_sem.at[j])

    def begin(j, carry):
        for copy in tile_copies(j):
            copy.start()
        for k, source in enumerate(orb_hbm):

            @pl.when(meta[4, j] == k)
            def _(source=source):
                orb_copy(j, source).start()

        return carry

    def work(j, carry):
        for copy in tile_copies(j):
            copy.wait()
        orb_copy(j, orb_hbm[0]).wait()
        masked = (tile[j] * mask_ref[j][None]).reshape(2 * size * 128, 128)
        product = jnp.dot(masked, orb[j], preferred_element_type=F32).astype(BF)
        result[j] = product.reshape(2 * size, 128, 128)
        group, entry = meta[0, j], meta[1, j]

        @pl.when(entry < MAIN)
        def _():
            a_copy(j, a_main.at[group, entry]).start()

        @pl.when(entry >= MAIN)
        def _():
            a_copy(j, a_extra.at[group, entry - MAIN]).start()

        piece, place = meta[2, j], meta[3, j]
        for s, target in enumerate(b_main):

            @pl.when(jnp.logical_and(piece == s, place < MAIN))
            def _(target=target):
                b_copy(j, target.at[place]).start()

        @pl.when(place >= MAIN)
        def _():
            b_copy(j, b_extra.at[piece, place - MAIN]).start()

        return carry

    def end(j, carry):
        a_copy(j, a_main.at[0, 0]).wait()
        b_copy(j, b_main[0].at[0]).wait()
        return carry

    lax.fori_loop(0, live[0], begin, 0)
    lax.fori_loop(0, live[0], work, 0)
    lax.fori_loop(0, live[0], end, 0)


def transform(first, size, meta, live, tiles, mask, orbitals):
    smem = pl.BlockSpec(memory_space=pltpu.SMEM)
    hbm = pl.BlockSpec(memory_space=pltpu.HBM)
    anywhere = pl.BlockSpec(memory_space=pl.ANY)
    vmem = pl.BlockSpec(memory_space=pltpu.VMEM)
    sems = pltpu.SemaphoreType.DMA((16,))
    shapes = [(4, MAIN), (4, 8 - MAIN), (4, 8 - MAIN)] + [(MAIN,)] * 4
    return pl.pallas_call(
        functools.partial(transform_kernel, first, size),
        in_specs=[smem, smem, hbm, vmem] + [anywhere] * 2,
        out_specs=[hbm] * 7,
        out_shape=[jax.ShapeDtypeStruct(shape + (size, 128, 128), BF) for shape in shapes],
        scratch_shapes=[
            pltpu.VMEM((16, 2 * size, 128, 128), BF),
            pltpu.VMEM((16, 128, 128), BF),
            pltpu.VMEM((16, 2 * size, 128, 128), BF),
            pltpu.SemaphoreType.DMA((2, 16)),
            sems,
            sems,
            sems,
        ],
        compiler_params=params(MOST),
        cost_estimate=cost(2 * 16 * 2 * size * 128**3, 16 * 2 * size * 2**16),
        name="transform",
    )(meta, live, tiles, mask, *orbitals)


def collect_kernel(along_x, size, codes, source, place, mine, *refs):
    if along_x:
        main, extra, outs, rest = refs[:4], refs[4], refs[5:9], refs[9:]
    else:
        main, extra, outs, rest = [refs[0].at[k] for k in range(4)], refs[1], refs[2:3], refs[3:]
    buffer, acc, result, table, count, in_sem, out_sem = rest

    def arrival(k, q, origin):
        return pltpu.make_async_copy(origin, buffer.at[k, q], in_sem.at[k, q])

    def departure(j, target):
        return pltpu.make_async_copy(result.at[j], target, out_sem.at[j])

    for k in range(SIDE):
        for t in range(SIDE):
            count[t] = 0
            for r in range(CAP):
                table[(k * SIDE + t) * CAP + r] = 0
        row = source[k]

        def visit(slot, q, k=k, row=row):
            code = codes[row, slot]
            owner = code // 4
            fixed, free = (owner // 4, owner % 4) if along_x else (owner % 4, owner // 4)
            hit = jnp.logical_and(code >= 0, fixed == mine[0])

            @pl.when(hit)
            def _():
                rank = jnp.minimum(count[free], CAP - 1)
                table[(k * SIDE + free) * CAP + rank] = q * 4 + code % 4 + 1
                count[free] = rank + 1

            @pl.when(jnp.logical_and(hit, q < MAIN))
            def _():
                arrival(k, q, main[k].at[q]).start()

            @pl.when(jnp.logical_and(hit, q >= MAIN))
            def _():
                arrival(k, q, extra.at[k, q - MAIN]).start()

            return q + hit.astype(jnp.int32)

        lax.fori_loop(0, 16, visit, jnp.int32(0))

    for j in range(SIDE):
        acc[...] = jnp.zeros(acc.shape, F32)
        for k in range(SIDE):
            for r in range(CAP):
                code = table[(k * SIDE + j) * CAP + r]

                @pl.when(code > 0)
                def _(k=k, code=code):
                    q, sub = (code - 1) // 4, (code - 1) % 4
                    arrival(k, q, main[k].at[0]).wait()
                    acc[sub] += buffer[k, q].astype(F32)

        for s in range(4):
            result[j, :, s * 128 : (s + 1) * 128, :] = acc[s].astype(BF)
        if along_x:
            for s in range(SIDE):

                @pl.when(place[j] == s)
                def _(s=s, j=j):
                    departure(j, outs[s]).start()

        else:
            departure(j, outs[0].at[j]).start()
    for j in range(SIDE):
        departure(j, outs[0] if along_x else outs[0].at[0]).wait()


def collect(along_x, size, codes, source, place, mine, main, extra):
    smem = pl.BlockSpec(memory_space=pltpu.SMEM)
    hbm = pl.BlockSpec(memory_space=pltpu.HBM)
    anywhere = pl.BlockSpec(memory_space=pl.ANY)
    out = (size, 512, 128)
    shapes = [jax.ShapeDtypeStruct(out, BF)] * 4 if along_x else [jax.ShapeDtypeStruct((4,) + out, BF)]
    return pl.pallas_call(
        functools.partial(collect_kernel, along_x, size),
        in_specs=[smem] * 4 + [anywhere] * (len(main) + 1),
        out_specs=[hbm] * len(shapes),
        out_shape=shapes,
        scratch_shapes=[
            pltpu.VMEM((SIDE, 8, size, 128, 128), BF),
            pltpu.VMEM((4, size, 128, 128), F32),
            pltpu.VMEM((SIDE,) + out, BF),
            pltpu.SMEM((4 * SIDE * CAP,), jnp.int32),
            pltpu.SMEM((SIDE,), jnp.int32),
            pltpu.SemaphoreType.DMA((SIDE, 8)),
            pltpu.SemaphoreType.DMA((SIDE,)),
        ],
        compiler_params=params(MOST),
        cost_estimate=cost(2**22, size * 3 * 2**19),
        name="collect",
    )(codes, source, place, mine, *main, extra)


def finish_kernel(size, first_ref, *refs):
    out_ref = refs[-1]
    for half in range(2):
        pieces = [first_ref[k] for k in range(4)] if half == 0 else [ref[...] for ref in refs[:4]]
        total = pieces[0].astype(F32)
        for piece in pieces[1:]:
            total += piece.astype(F32)
        for p in range(size):
            turned = total[p].T.astype(BF)
            out_ref[:, size * half + p] = turned.reshape(8, 16, 128)


def finish(size, first, pieces):
    return pl.pallas_call(
        functools.partial(finish_kernel, size),
        grid=(4,),
        in_specs=[pl.BlockSpec((4, size, 128, 128), lambda m: (0, 0, m, 0))]
        + [pl.BlockSpec((size, 128, 128), lambda m: (0, m, 0))] * 4,
        out_specs=pl.BlockSpec((8, 2 * size, 16, 128), lambda m: (0, 0, 0, m)),
        out_shape=jax.ShapeDtypeStruct((8, 2 * size, 16, 512), BF),
        compiler_params=params(),
        cost_estimate=cost(2**21, 5 * 2**20),
        name="finish",
    )(first, *pieces)


def product_kernel(rows_cut, columns_cut, has_add, filled, zsel, way, *refs):
    refs, count = list(refs), len(columns_cut)

    def halves(cut):
        if cut:
            return refs.pop(0), refs.pop(0)
        ref = refs.pop(0)
        half = ref.shape[0] // 2
        return ref.at[pl.ds(0, half)], ref.at[pl.ds(half, half)]

    rows_hbm = [halves(cut) for cut in rows_cut]
    columns_hbm = [halves(cut) for cut in columns_cut]
    if has_add:
        add_hbm, refs = refs[0], refs[1 + filled :]
        outs, refs = refs[:SIDE], refs[SIDE:]
    else:
        outs, refs = refs[:1], refs[1:]
    left, right, result, left_sem, right_sem, out_sem, *more = refs

    def left_copy(h, source):
        return pltpu.make_async_copy(source[h], left.at[pl.ds(256 * h, 256)], left_sem.at[h])

    def right_copy(h, n):
        return pltpu.make_async_copy(
            columns_hbm[n][h], right.at[n, pl.ds(512 * h, 512)], right_sem.at[h, n]
        )

    def out_copy(n, target):
        return pltpu.make_async_copy(result.at[n], target, out_sem.at[n])

    def add_copy(n):
        return pltpu.make_async_copy(add_hbm.at[n], more[0].at[n], more[1].at[n])

    for k, source in enumerate(rows_hbm):

        @pl.when(zsel[0] == k)
        def _(source=source):
            for h in range(2):
                left_copy(h, source).start()

    for n in range(count):
        for h in range(2):
            right_copy(h, n).start()
        if has_add:
            add_copy(n).start()
    for h in range(2):
        left_copy(h, rows_hbm[0]).wait()
    for n in range(count):
        for h in range(2):
            right_copy(h, n).wait()
        value = jnp.dot(left[...], right[n], preferred_element_type=F32)
        if has_add:
            add_copy(n).wait()
            value += more[0][n].astype(F32)
        result[n] = value.astype(BF)
        if has_add:
            for s in range(SIDE):

                @pl.when(way[n] == s)
                def _(n=n, s=s):
                    out_copy(n, outs[s]).start()

        else:
            out_copy(n, outs[0].at[n]).start()
    for n in range(count):
        out_copy(n, outs[0] if has_add else outs[0].at[0]).wait()


def product(zsel, way, rows, columns, add=None, fill=()):
    smem = pl.BlockSpec(memory_space=pltpu.SMEM)
    anywhere = pl.BlockSpec(memory_space=pl.ANY)
    has_add, count = add is not None, len(columns)
    tiles = (count, 512, 512)
    sems = pltpu.SemaphoreType.DMA((count,))
    scratch = [
        pltpu.VMEM((512, 1024), BF),
        pltpu.VMEM((count, 1024, 512), BF),
        pltpu.VMEM(tiles, BF),
        pltpu.SemaphoreType.DMA((2,)),
        pltpu.SemaphoreType.DMA((2, count)),
        sems,
    ]
    cuts = [[isinstance(array, tuple) for array in arrays] for arrays in (rows, columns)]
    operands = []
    for array in [*rows, *columns]:
        operands += array if isinstance(array, tuple) else (array,)
    aliases = {}
    if has_add:
        aliases = {3 + len(operands) + n: n for n in range(len(fill))}
        operands += [add, *fill]
        scratch += [pltpu.VMEM(tiles, BF), sems]
        out_shape = [jax.ShapeDtypeStruct((512, 512), BF)] * SIDE
    else:
        out_shape = [jax.ShapeDtypeStruct(tiles, BF)]
    return pl.pallas_call(
        functools.partial(product_kernel, *cuts, has_add, len(fill)),
        in_specs=[smem] * 2 + [anywhere] * len(operands),
        out_specs=[anywhere] * len(out_shape),
        out_shape=out_shape,
        scratch_shapes=scratch,
        input_output_aliases=aliases,
        compiler_params=params(MOST),
        cost_estimate=cost(count * 2 * 512 * 512 * 1024, (1 + 2 * count) * 2**20),
        name="product",
    )(zsel, way, *operands)


def per_device(
    three_index, pair_mask, pair_owner, pair_sub, pair_nu, live_count, coefficients, fit_matrix
):
    slots = three_index.shape[0]
    x, z, y, c = (lax.axis_index(name) for name in ("x", "z", "y", "c"))

    swapped_fit = lax.ppermute(fit_matrix, "c", [(0, 1), (1, 0)])
    pair_fit = jnp.where(
        c == 0,
        jnp.concatenate([fit_matrix, swapped_fit], 0),
        jnp.concatenate([swapped_fit, fit_matrix], 0),
    )
    fits = jnp.stack([pair_fit] + [shifted(pair_fit, "y", s) for s in (1, 2, 3)])
    fit = fits[(y - jnp.arange(4)) % 4].reshape(64, 64)

    alive = jnp.arange(slots) < live_count[0]
    code = jnp.where(alive, pair_owner[:, 0] * 4 + pair_sub, -1).astype(BF)
    half_blocks = lax.dynamic_slice_in_dim(coefficients, c * 256, 256, 0)
    code_rows = jnp.broadcast_to(jnp.pad(code, (0, 112))[None], (16, 128))
    sent = jnp.concatenate([half_blocks, code_rows], 0)
    swap = [(0, 1), (1, 0)]
    own = lax.all_to_all(
        jnp.broadcast_to(sent[None], (16, 272, 128)), ("x", "z"), 0, 0, tiled=True
    )

    where = jnp.stack([x, z, c]).astype(jnp.int32)
    meta = plan(where, pair_owner, pair_nu)
    mask = jnp.repeat(jnp.repeat(pair_mask, 16, 1), 16, 2).astype(BF)
    own, mask, fit, meta = lax.optimization_barrier((own, mask, fit, meta))
    orbitals = [own, lax.ppermute(own, "c", swap)]
    codes = own[:, 256, :slots].astype(jnp.int32)

    steps = jnp.arange(4, dtype=jnp.int32)
    to_x, to_z = codes // 16, codes // 4 % 4
    from_x, from_z = jnp.repeat(steps, 4), jnp.tile(steps, 4)

    def lengths(to, origin):
        hits = (codes[..., None] >= 0) & (to[..., None] == steps) & (to != origin[:, None])[..., None]
        return jnp.max(jnp.sum(hits.astype(jnp.int32), 1))

    overflow = jnp.maximum(lengths(to_x, from_x), lengths(to_z, from_z)) > MAIN

    size = 4

    spot = jnp.arange(1024)
    spread = (spot[:, None] // 16 == jnp.arange(64)[None, :]).astype(BF)
    mixing = jnp.dot(jnp.dot(spread, fit, preferred_element_type=F32).astype(BF), spread.T)
    same = spot[:, None] % 16 == spot[None, :] % 16
    mixing = jnp.where(same, mixing, 0).astype(BF)

    a_main, a_extra, b_extra, *b_main = transform(
        0, size, meta, live_count, three_index, mask, orbitals
    )
    a_got = lax.all_to_all(a_main, "z", 0, 0, tiled=True)
    b_got = [b_main[0]] + [shifted(b_main[s], "x", s) for s in (1, 2, 3)]
    a_got, *b_got = lax.optimization_barrier((a_got, *b_got))

    def send_extra(a, b):
        moved = [b[:1]] + [shifted(b[s : s + 1], "x", s) for s in (1, 2, 3)]
        return lax.all_to_all(a, "z", 0, 0, tiled=True), jnp.concatenate(moved, 0)

    a_extra, b_extra = lax.cond(overflow, send_extra, lambda a, b: (a, b), a_extra, b_extra)
    (a_sum,) = collect(False, size, codes, x * 4 + steps, steps, z[None], [a_got], a_extra)
    a_last = lax.all_to_all(a_sum, "x", 0, 0, tiled=True)
    b_sum = collect(
        True, size, codes, (x - steps) % 4 * 4 + z, (steps - z) % 4, x[None], b_got, b_extra
    )
    b_last = [b_sum[0]] + [shifted(b_sum[s], "z", s) for s in (1, 2, 3)]

    cut = finish(size, a_last, b_last)
    rows = lax.all_to_all(cut, ("y", "c"), 0, 0, tiled=True).reshape(1024, 512)
    turned = rows.T
    beside = [shifted(turned, "z", s) for s in (1, 3)]
    fitted = jnp.dot(mixing, rows, preferred_element_type=F32).astype(BF)
    early = [fitted] + [shifted(fitted, "x", s) for s in (1, 3)]
    *beside, early_next, early_last = lax.optimization_barrier((*beside, early[1], early[2]))
    early = [fitted, early_next, early_last]
    onward = (early[1][:512], early[2][512:], beside[0][:256], beside[1][256:])
    *onward, early[0] = lax.optimization_barrier((*onward, fitted))
    late = [(shifted(onward[0], "x", 1), shifted(onward[1], "x", 3))]
    across = [turned, (shifted(onward[2], "z", 1), shifted(onward[3], "z", 3))]

    def choose(owner, turn):
        return ((z - 2 * owner - turn) % 4 // 2)[None]

    way = ((x - y - jnp.array([0, 1, 3, 2])) % 4).astype(jnp.int32)
    turn = (z + 1) % 2
    other, mine = choose(1 - c, turn), choose(c, turn)
    (part,) = product(other, way, beside, early)
    part = lax.ppermute(part, "c", swap)
    tiles = product(mine, way[:3], beside, early, part)
    *tiles, top, bottom, low, high = lax.optimization_barrier((*tiles, *late[0], *across[1]))
    late, across = [(top, bottom)], [turned, (low, high)]
    (part,) = product(other, way, beside, late)
    part = lax.ppermute(part, "c", swap)
    odd = product(mine, way[3:], beside, late, part, tiles)

    turn = z % 2
    other, mine = choose(1 - c, turn), choose(c, turn)
    other, *odd = lax.optimization_barrier((other, *odd))
    (part,) = product(other, way, across, early + late)
    part = lax.ppermute(part, "c", swap)
    even = product(mine, way, across, early + late, part)
    got = [None, None]
    for t, tiles in ((1, odd), (0, even)):
        parts = [tiles[0]] + [shifted(tiles[s], "y", s) for s in (1, 2, 3)]
        tile = sum(part.astype(F32) for part in parts).astype(BF)
        pairs = [
            (zz * 2 + k, (2 * k + (zz + t) % 2) * 2 + zz // 2) for zz in range(4) for k in range(2)
        ]
        got[t] = lax.ppermute(tile, ("z", "c"), pairs).astype(F32)
    scale = 8192 ** (-0.5)
    level = z % 2 == 0
    first = jnp.where(level, got[0], got[1]) * scale
    second = jnp.where(level, got[1], got[0]) * scale
    return jnp.concatenate([first, second], 1)


def solution(mesh):
    grid = Mesh(mesh.devices.reshape(4, 4, 4, 2), ("x", "z", "y", "c"))
    atom, aux = ("x", "z"), ("y", "c")
    in_specs = (
        P(atom, aux, None, None),
        P(atom, None, None),
        P(atom, None),
        P(atom),
        P(atom),
        P(atom),
        P(atom, None),
        P(aux, None),
    )
    return jax.shard_map(
        per_device, mesh=grid, in_specs=in_specs, out_specs=P(atom, aux), check_vma=False
    )
```
